32 devices in a mesh: groups: 2 (over x), expert: 16 (over z, y, core).
Axes of the slice: x: 2, y: 2, z: 4, core: 2. Of those that a mesh axis runs over, the one named last changes fastest.
Arguments:
- tokens: bfloat16 [4096, 4096], P(('groups', 'expert')), parts along dimension 0, may hold values from -6 to 6
- gate_weight: bfloat16 [16, 4096, 1536], P('expert'), may hold values from -0.09375 to 0.09375
- up_weight: bfloat16 [16, 4096, 1536], P('expert'), may hold values from -0.09375 to 0.09375
- down_weight: bfloat16 [16, 1536, 4096], P('expert'), may hold values from -0.15625 to 0.15625
- expert_ids: int32 [4096, 8], P(('groups', 'expert')), parts along dimension 0, may hold values from 0 to 127, as said below
- slots: int32 [4096, 8], P(('groups', 'expert')), parts along dimension 0, may hold values from -1 to 15, as said below
- gates: float32 [4096, 8], P(('groups', 'expert')), parts along dimension 0, may hold values from 0.25 to 2.5
Outputs:
- mixed: bfloat16 [4096, 4096], P(('groups', 'expert')), parts along dimension 0
The draws below stay inside these ranges and needn't reach their ends.
There are 2 independent parts, one for each index of `groups`. The reference program is written for one: setup_inputs(seed, part) draws one part's arguments, and reference() takes and returns one part's arrays. A program takes and returns all parts, laid end to end along the dimension named above; an argument that names none is the same for every part. Nothing has to cross between parts.
Inputs may be any that keep to these rules, and one draw needn't show every extreme that they name: `expert_ids`: each row names 8 different experts. Only experts 0 to 15 are computed here. Pairs are ranked in the order of rows, then of the 8 choices. A pair has slot -1 if its expert is 16 or above, or if 16 earlier pairs of the rows of the same device name its expert; else its slot is the number of such earlier pairs. So the slots of one expert on one device are 0, 1, ... without gaps. In every draw some expert has all 16 slots filled on every device.
All inputs are finite; a program needn't handle non-finite values.
Results may differ from the reference program's by a relative error of at most 0.0058.
Values may be sent and summed in bfloat16 or wider, within the bound.
A program may use at most 128 MiB of HBM per device.

```python
import math
import jax
import jax.numpy as jnp
from jax import lax

D = 4096
FF = 1536
GATING_SPECIALS = 128
TOP = 8
EXPERTS = 16
TOK_DEV = 128
TOKENS = 2048
CAP = 16
FF_DEV = 1536
N_EXPERT = 16


def route_choice(key):
    noise_seeds = jax.random.split(key, 4)
    drawn_affinity = jax.random.randint(noise_seeds[0], (TOKENS, GATING_SPECIALS), 0, 1 << 20)
    extra_lift = jax.random.randint(noise_seeds[1], (GATING_SPECIALS,), 0, 1 << 19)
    hottest = jax.random.randint(noise_seeds[2], (), 0, EXPERTS)
    blocks = TOKENS // TOK_DEV
    orders = jax.vmap(lambda sub_key: jax.random.permutation(sub_key, TOK_DEV))(jax.random.split(noise_seeds[3], blocks)).reshape(TOKENS)
    forced = orders < CAP
    matrix_lane = jnp.arange(GATING_SPECIALS, dtype=jnp.int32)
    lift_multiplier = jnp.where(forced[:, None] & (matrix_lane[None, :] == hottest), 1 << 21, 0)
    gating_affinity = (drawn_affinity + extra_lift[None, :] + lift_multiplier) * GATING_SPECIALS + matrix_lane[None, :]
    gating_affinity = gating_affinity.astype(jnp.int32)
    _, chosen = lax.top_k(gating_affinity, TOP)
    return chosen.astype(jnp.int32)


def rank_slots(chosen):
    blocks = TOKENS // TOK_DEV
    flat = chosen.reshape(blocks, TOK_DEV * TOP)
    onehot = (flat[:, :, None] == jnp.arange(EXPERTS, dtype=jnp.int32)[None, None, :]).astype(jnp.int32)
    before = jnp.cumsum(onehot, axis=1) - onehot
    ranked = jnp.sum(before * onehot, axis=2)
    usable = (flat < EXPERTS) & (ranked < CAP)
    return jnp.where(usable, ranked, -1).reshape(TOKENS, TOP).astype(jnp.int32)


def draw_expert_ids(key, part):
    chosen = route_choice(key)
    return chosen


def draw_slots(key, part):
    chosen = route_choice(key)
    return rank_slots(chosen)


def block_scale(rng, dims, cuts, smallest, top_value):
    gain, own = 1.0, jax.random.fold_in(rng, 6)
    for dim, blocks in cuts:
        steps = jnp.exp(jax.random.uniform(jax.random.fold_in(own, dim), (blocks,), jnp.float32, smallest / len(cuts), top_value / len(cuts)))
        gain = gain * jnp.repeat(steps, dims[dim] // blocks).reshape([-1 if axis == dim else 1 for axis in range(len(dims))])
    return gain


def noise(rng, shape, width, bound, cuts=(), kind=jnp.bfloat16):
    values = jax.random.normal(rng, shape, jnp.float32) * width
    if len(cuts) > 0:
        values = block_scale(rng, shape, cuts, -0.22, 0.18) * values
    return jnp.clip(values, min=-bound, max=bound).astype(kind)


def setup_inputs(seed: int = 0, part: int = 0) -> dict:
    streams_of = jax.random.split(jax.random.key(seed), 8)
    part_keys = jax.random.split(jax.random.fold_in(streams_of[7], part), 8)
    return {
        "tokens": noise(part_keys[0], (TOKENS, D), 1.0, 6.0, ((0, 16),)),
        "gate_weight": noise(streams_of[1], (N_EXPERT, D, FF_DEV), D ** -0.5, 0.09375, ((0, 16),)),
        "up_weight": noise(streams_of[2], (N_EXPERT, D, FF_DEV), D ** -0.5, 0.09375, ((0, 16),)),
        "down_weight": noise(streams_of[3], (N_EXPERT, FF_DEV, D), FF ** -0.5, 0.15625, ((0, 16),)),
        "expert_ids": draw_expert_ids(jax.random.fold_in(jax.random.fold_in(streams_of[7], part), 71), part),
        "slots": draw_slots(jax.random.fold_in(jax.random.fold_in(streams_of[7], part), 71), part),
        "gates": jnp.clip(jnp.exp(math.log(2.5) - 2.3025851 * jax.random.uniform(part_keys[6], (TOKENS, TOP), jnp.float32) ** block_scale(part_keys[6], (TOKENS, TOP), ((0, 16),), -0.2, 0.2)), 0.25, 2.5),
    }


def reference(tokens, gate_weight, up_weight, down_weight, expert_ids, slots, gates):
    token_count = tokens.shape[0]
    model_width = tokens.shape[1]
    blocks = token_count // TOK_DEV
    shards = N_EXPERT // EXPERTS
    ff_dev = gate_weight.shape[2]
    pair_token = jnp.broadcast_to(jnp.arange(token_count, dtype=jnp.int32)[:, None], expert_ids.shape)
    filled = slots >= 0
    region = EXPERTS * blocks * CAP
    target = jnp.where(filled, (expert_ids * blocks + pair_token // TOK_DEV) * CAP + slots, region).astype(jnp.int32)
    source_row = jnp.full((region + 1,), token_count, jnp.int32).at[target.reshape(-1)].set(pair_token.reshape(-1))[:region]
    padded = jnp.concatenate([tokens, jnp.zeros((1, model_width), tokens.dtype)], axis=0)
    slot_rows = padded[source_row].reshape(EXPERTS, blocks * CAP, model_width)
    gate_parts = gate_weight.reshape(EXPERTS, shards, model_width, ff_dev)
    up_parts = up_weight.reshape(EXPERTS, shards, model_width, ff_dev)
    down_parts = down_weight.reshape(EXPERTS, shards, ff_dev, model_width)

    def one_expert(operands):
        rows_e, gate_e, up_e, down_e = operands
        summed = jnp.zeros((rows_e.shape[0], model_width), jnp.float32)
        for shard_id in range(shards):
            gate_val = jnp.dot(rows_e, gate_e[shard_id], preferred_element_type=jnp.float32)
            up_val = jnp.dot(rows_e, up_e[shard_id], preferred_element_type=jnp.float32)
            hidden = (jax.nn.silu(gate_val) * up_val).astype(jnp.bfloat16)
            partial_value = jnp.dot(hidden, down_e[shard_id], preferred_element_type=jnp.float32).astype(jnp.bfloat16)
            summed = summed + partial_value.astype(jnp.float32)
        return summed

    expert_out = lax.map(one_expert, (slot_rows, gate_parts, up_parts, down_parts)).reshape(region, model_width)
    combined = jnp.zeros((token_count, model_width), jnp.float32)
    for matrix_lane in range(expert_ids.shape[1]):
        picked = jnp.minimum(target[:, matrix_lane], region - 1)
        combined = combined + jnp.where(filled[:, matrix_lane, None], gates[:, matrix_lane, None] * expert_out[picked], 0.0)
    return combined.astype(jnp.bfloat16)
```

```python
import functools

import jax
import jax.numpy as jnp
from jax import lax
from jax.experimental import pallas as pl
from jax.experimental.pallas import tpu as pltpu
from jax.sharding import PartitionSpec as P

EXPERTS = 16
CAP = 16
GROUPS = 4
ORDER = (2, 3, 1, 0)


def xor_index(a, b, n):
    out, bit = 0, 1
    while bit < n:
        out = out + ((a // bit + b // bit) % 2) * bit
        bit *= 2
    return out


def column_tile(width, most):
    tile = most
    while width % tile:
        tile //= 2
    return tile


def kernel(
    n, tokens_ref, ids_ref, slots_ref, gates_ref, gate_hbm, up_hbm, down_hbm, out_ref,
    gate_w, up_w, down_w, send, inbox, outbox, back, hidden, acc, pack, weight_sems,
    there_send, there_recv, back_send, back_recv,
):
    me = lax.axis_index("expert")
    shards = n // EXPERTS
    per_group = n // GROUPS
    rows = per_group * CAP
    token_count, width = tokens_ref.shape
    ff = gate_w.shape[1]
    top = ids_ref.shape[1]

    weights = [
        pltpu.make_async_copy(src.at[0], dst, weight_sems.at[i])
        for i, (src, dst) in enumerate(((gate_hbm, gate_w), (up_hbm, up_w), (down_hbm, down_w)))
    ]
    for copy in weights:
        copy.start()

    barrier = pltpu.get_barrier_semaphore()

    def greet(j, carry):
        pl.semaphore_signal(barrier, inc=1, device_id={"expert": xor_index(me, j, n)})
        return carry

    lax.fori_loop(1, n, greet, 0)

    target = jnp.where(slots_ref[...] >= 0, ids_ref[...] * CAP + slots_ref[...], -1)
    lane = lax.broadcasted_iota(jnp.int32, (token_count, EXPERTS * CAP), 1)
    chosen = jnp.zeros((token_count, EXPERTS * CAP), jnp.float32)
    for k in range(top):
        chosen = jnp.where(target[:, k : k + 1] == lane, 1.0, chosen)
    pack[...] = chosen.T.astype(jnp.bfloat16)
    tile_p = column_tile(width, 512)

    def pack_tile(i, carry):
        cols = pl.ds(pl.multiple_of(i * tile_p, tile_p), tile_p)
        send[:, cols] = jnp.dot(
            pack[...], tokens_ref[:, cols], preferred_element_type=jnp.float32
        ).astype(jnp.bfloat16)
        return carry

    lax.fori_loop(0, width // tile_p, pack_tile, 0)
    pl.semaphore_wait(barrier, n - 1)

    def block(j):
        return pl.ds(pl.multiple_of(j * CAP, CAP), CAP)

    def dispatch(j):
        peer = xor_index(me, j, n)
        return pltpu.make_async_remote_copy(
            src_ref=send.at[block(peer // shards)],
            dst_ref=inbox.at[block(j)],
            send_sem=there_send.at[j],
            recv_sem=there_recv.at[j],
            device_id={"expert": peer},
        )

    def giveback(j):
        return pltpu.make_async_remote_copy(
            src_ref=outbox.at[block(j)],
            dst_ref=back.at[block(j)],
            send_sem=back_send.at[j],
            recv_sem=back_recv.at[j],
            device_id={"expert": xor_index(me, j, n)},
        )

    def each(group, act):
        first = max(group * per_group, 1)

        def step(j, carry):
            act(j)
            return carry

        lax.fori_loop(first, (group + 1) * per_group, step, 0)

    for group in ORDER:
        each(group, lambda j: dispatch(j).start())
    inbox[0:CAP, :] = send[block(me // shards), :]

    tile_f = column_tile(ff, 256)
    tile_d = column_tile(width, 512)
    for place, group in enumerate(ORDER):
        mine = slice(group * rows, (group + 1) * rows)
        each(group, lambda j: dispatch(j).wait_recv())
        if place == 0:
            weights[0].wait()
            weights[1].wait()

        def first_half(i, carry):
            cols = pl.ds(pl.multiple_of(i * tile_f, tile_f), tile_f)
            gate_val = jnp.dot(
                inbox[mine, :], gate_w[:, cols], preferred_element_type=jnp.float32
            )
            up_val = jnp.dot(inbox[mine, :], up_w[:, cols], preferred_element_type=jnp.float32)
            hidden[:, cols] = (jax.nn.silu(gate_val) * up_val).astype(jnp.bfloat16)
            return carry

        lax.fori_loop(0, ff // tile_f, first_half, 0)
        if place == 0:
            weights[2].wait()

        def second_half(i, carry):
            cols = pl.ds(pl.multiple_of(i * tile_d, tile_d), tile_d)
            outbox[mine, cols] = jnp.dot(
                hidden[...], down_w[:, cols], preferred_element_type=jnp.float32
            ).astype(jnp.bfloat16)
            return carry

        lax.fori_loop(0, width // tile_d, second_half, 0)
        each(group, lambda j: giveback(j).start())
    back[0:CAP, :] = outbox[0:CAP, :]

    def mix_group(place, group):
        mine = slice(group * rows, (group + 1) * rows)
        column = lax.broadcasted_iota(jnp.int32, (token_count, rows), 1) + group * rows
        expert = ((column // CAP) ^ me) // shards
        key = expert * CAP + column % CAP
        mix = jnp.zeros((token_count, rows), jnp.float32)
        for k in range(top):
            mix = jnp.where(target[:, k : k + 1] == key, gates_ref[:, k : k + 1], mix)
        high = mix.astype(jnp.bfloat16)
        low = (mix - high.astype(jnp.float32)).astype(jnp.bfloat16)
        both = jnp.concatenate([high, low], axis=0)
        each(group, lambda j: giveback(j).wait_recv())

        def mix_tile(i, carry):
            cols = pl.ds(pl.multiple_of(i * tile_d, tile_d), tile_d)
            product = jnp.dot(both, back[mine, cols], preferred_element_type=jnp.float32)
            total = product[:token_count] + product[token_count:]
            if place > 0:
                total = total + acc[:, cols]
            if place < GROUPS - 1:
                acc[:, cols] = total
            else:
                out_ref[:, cols] = total.astype(jnp.bfloat16)
            return carry

        lax.fori_loop(0, width // tile_d, mix_tile, 0)

    for place, group in enumerate((0, 1, 2, 3)):
        mix_group(place, group)
    for group in range(GROUPS):
        each(group, lambda j: dispatch(j).wait_send())
        each(group, lambda j: giveback(j).wait_send())


def body(tokens, gate_weight, up_weight, down_weight, expert_ids, slots, gates):
    n = lax.axis_size("expert")
    token_count, width = tokens.shape
    ff = gate_weight.shape[2]
    rows = n // GROUPS * CAP
    vmem = pl.BlockSpec(memory_space=pltpu.VMEM)
    hbm = pl.BlockSpec(memory_space=pl.ANY)
    return pl.pallas_call(
        functools.partial(kernel, n),
        out_shape=jax.ShapeDtypeStruct((token_count, width), jnp.bfloat16),
        in_specs=[vmem] * 4 + [hbm] * 3,
        out_specs=vmem,
        scratch_shapes=[
            pltpu.VMEM((width, ff), jnp.bfloat16),
            pltpu.VMEM((width, ff), jnp.bfloat16),
            pltpu.VMEM((ff, width), jnp.bfloat16),
            pltpu.VMEM((EXPERTS * CAP, width), jnp.bfloat16),
            pltpu.VMEM((n * CAP, width), jnp.bfloat16),
            pltpu.VMEM((n * CAP, width), jnp.bfloat16),
            pltpu.VMEM((n * CAP, width), jnp.bfloat16),
            pltpu.VMEM((rows, ff), jnp.bfloat16),
            pltpu.VMEM((token_count, width), jnp.float32),
            pltpu.VMEM((EXPERTS * CAP, token_count), jnp.bfloat16),
            pltpu.SemaphoreType.DMA((3,)),
            pltpu.SemaphoreType.DMA((n,)),
            pltpu.SemaphoreType.DMA((n,)),
            pltpu.SemaphoreType.DMA((n,)),
            pltpu.SemaphoreType.DMA((n,)),
        ],
        compiler_params=pltpu.CompilerParams(
            collective_id=0, has_side_effects=True, vmem_limit_bytes=58 * 1024 * 1024
        ),
        name="expert_layer",
    )(tokens, expert_ids, slots, gates, gate_weight, up_weight, down_weight)


def solution(mesh):
    return jax.shard_map(
        body,
        mesh=mesh,
        in_specs=(
            P(("groups", "expert"), None),
            P("expert", None, None),
            P("expert", None, None),
            P("expert", None, None),
            P(("groups", "expert"), None),
            P(("groups", "expert"), None),
            P(("groups", "expert"), None),
        ),
        out_specs=P(("groups", "expert"), None),
        check_vma=False,
    )
```

```python
import functools

import jax
import jax.numpy as jnp
from jax import lax
from jax.experimental import pallas as pl
from jax.experimental.pallas import tpu as pltpu
from jax.sharding import PartitionSpec as P

EXPERTS = 16
CAP = 16
SENDS = ((8, 8), (4, 4), (0, 4))
WORKS = ((8, 4), (0, 8), (12, 2), (14, 2))
MIXES = ((0, 8), (8, 4), (12, 4))


def xor_index(a, b, n):
    out, bit = 0, 1
    while bit < n:
        out = out + ((a // bit + b // bit) % 2) * bit
        bit *= 2
    return out


def column_tile(width, most):
    tile = most
    while width % tile:
        tile //= 2
    return tile


def kernel(
    n, tokens_ref, ids_ref, slots_ref, gates_ref, gate_hbm, up_hbm, down_hbm, out_ref,
    gate_w, up_w, down_w, send, inbox, outbox, back, hidden, acc, pack, weight_sems,
    there_send, there_recv, back_send, back_recv,
):
    me = lax.axis_index("expert")
    shards = n // EXPERTS
    unit = n // EXPERTS
    token_count, width = tokens_ref.shape
    ff = gate_w.shape[1]
    top = ids_ref.shape[0]

    weights = [
        pltpu.make_async_copy(src.at[0], dst, weight_sems.at[i])
        for i, (src, dst) in enumerate(((gate_hbm, gate_w), (up_hbm, up_w), (down_hbm, down_w)))
    ]
    for copy in weights:
        copy.start()

    barrier = pltpu.get_barrier_semaphore()

    def greet(j, carry):
        pl.semaphore_signal(barrier, inc=1, device_id={"expert": xor_index(me, j, n)})
        return carry

    lax.fori_loop(1, n, greet, 0)

    target = jnp.where(slots_ref[...] >= 0, ids_ref[...] * CAP + slots_ref[...], -1)
    slot_row = lax.broadcasted_iota(jnp.int32, (EXPERTS * CAP, token_count), 0)
    chosen = jnp.zeros((EXPERTS * CAP, token_count), jnp.float32)
    for k in range(top):
        chosen = jnp.where(target[k : k + 1, :] == slot_row, 1.0, chosen)
    pack[...] = chosen.astype(jnp.bfloat16)
    tile_p = column_tile(width, 512)

    def pack_tile(i, carry):
        cols = pl.ds(pl.multiple_of(i * tile_p, tile_p), tile_p)
        send[:, cols] = jnp.dot(
            pack[...], tokens_ref[:, cols], preferred_element_type=jnp.float32
        ).astype(jnp.bfloat16)
        return carry

    lax.fori_loop(0, width // tile_p, pack_tile, 0)
    pl.semaphore_wait(barrier, n - 1)

    def block(j):
        return pl.ds(pl.multiple_of(j * CAP, CAP), CAP)

    def dispatch(j):
        peer = xor_index(me, j, n)
        return pltpu.make_async_remote_copy(
            src_ref=send.at[block(peer // shards)],
            dst_ref=inbox.at[block(j)],
            send_sem=there_send.at[j],
            recv_sem=there_recv.at[j],
            device_id={"expert": peer},
        )

    def giveback(j):
        return pltpu.make_async_remote_copy(
            src_ref=outbox.at[block(j)],
            dst_ref=back.at[block(j)],
            send_sem=back_send.at[j],
            recv_sem=back_recv.at[j],
            device_id={"expert": xor_index(me, j, n)},
        )

    def each(group, act):
        first, count = group[0] * unit, group[1] * unit

        def step(j, carry):
            act(j)
            return carry

        lax.fori_loop(max(first, 1), first + count, step, 0)

    for group in SENDS:
        each(group, lambda j: dispatch(j).start())
    inbox[0:CAP, :] = send[block(me // shards), :]

    tile_f = column_tile(ff, 256)
    tile_d = column_tile(width, 512)
    for place, group in enumerate(WORKS):
        start, rows = group[0] * unit * CAP, group[1] * unit * CAP
        mine = slice(start, start + rows)
        each(group, lambda j: dispatch(j).wait_recv())
        if place == 0:
            weights[0].wait()
            weights[1].wait()

        def first_half(i, carry):
            cols = pl.ds(pl.multiple_of(i * tile_f, tile_f), tile_f)
            gate_val = jnp.dot(
                inbox[mine, :], gate_w[:, cols], preferred_element_type=jnp.float32
            )
            up_val = jnp.dot(inbox[mine, :], up_w[:, cols], preferred_element_type=jnp.float32)
            hidden[:rows, cols] = (jax.nn.silu(gate_val) * up_val).astype(jnp.bfloat16)
            return carry

        lax.fori_loop(0, ff // tile_f, first_half, 0)
        if place == 0:
            weights[2].wait()

        def second_half(i, carry):
            cols = pl.ds(pl.multiple_of(i * tile_d, tile_d), tile_d)
            outbox[mine, cols] = jnp.dot(
                hidden[:rows, :], down_w[:, cols], preferred_element_type=jnp.float32
            ).astype(jnp.bfloat16)
            return carry

        lax.fori_loop(0, width // tile_d, second_half, 0)
        each(group, lambda j: giveback(j).start())
    back[0:CAP, :] = outbox[0:CAP, :]

    def mix_group(place, group):
        start, rows = group[0] * unit * CAP, group[1] * unit * CAP
        mine = slice(start, start + rows)
        row = lax.broadcasted_iota(jnp.int32, (rows, token_count), 0) + start
        expert = ((row // CAP) ^ me) // shards
        key = expert * CAP + row % CAP
        mix = jnp.zeros((rows, token_count), jnp.float32)
        for k in range(top):
            mix = jnp.where(target[k : k + 1, :] == key, gates_ref[k : k + 1, :], mix)
        mix = mix.T
        high = mix.astype(jnp.bfloat16)
        low = (mix - high.astype(jnp.float32)).astype(jnp.bfloat16)
        both = jnp.concatenate([high, low], axis=0)
        each(group, lambda j: giveback(j).wait_recv())

        def mix_tile(i, carry):
            cols = pl.ds(pl.multiple_of(i * tile_d, tile_d), tile_d)
            product = jnp.dot(both, back[mine, cols], preferred_element_type=jnp.float32)
            total = product[:token_count] + product[token_count:]
            if place > 0:
                total = total + acc[:, cols]
            if place < len(MIXES) - 1:
                acc[:, cols] = total
            else:
                out_ref[:, cols] = total.astype(jnp.bfloat16)
            return carry

        lax.fori_loop(0, width // tile_d, mix_tile, 0)

    for place, group in enumerate(MIXES):
        mix_group(place, group)
    each((0, EXPERTS), lambda j: dispatch(j).wait_send())
    each((0, EXPERTS), lambda j: giveback(j).wait_send())


def body(tokens, gate_weight, up_weight, down_weight, expert_ids, slots, gates):
    n = lax.axis_size("expert")
    token_count, width = tokens.shape
    ff = gate_weight.shape[2]
    rows = max(count for _, count in WORKS) * (n // EXPERTS) * CAP
    vmem = pl.BlockSpec(memory_space=pltpu.VMEM)
    hbm = pl.BlockSpec(memory_space=pl.ANY)
    return pl.pallas_call(
        functools.partial(kernel, n),
        out_shape=jax.ShapeDtypeStruct((token_count, width), jnp.bfloat16),
        in_specs=[vmem] * 4 + [hbm] * 3,
        out_specs=vmem,
        scratch_shapes=[
            pltpu.VMEM((width, ff), jnp.bfloat16),
            pltpu.VMEM((width, ff), jnp.bfloat16),
            pltpu.VMEM((ff, width), jnp.bfloat16),
            pltpu.VMEM((EXPERTS * CAP, width), jnp.bfloat16),
            pltpu.VMEM((n * CAP, width), jnp.bfloat16),
            pltpu.VMEM((n * CAP, width), jnp.bfloat16),
            pltpu.VMEM((n * CAP, width), jnp.bfloat16),
            pltpu.VMEM((rows, ff), jnp.bfloat16),
            pltpu.VMEM((token_count, width), jnp.float32),
            pltpu.VMEM((EXPERTS * CAP, token_count), jnp.bfloat16),
            pltpu.SemaphoreType.DMA((3,)),
            pltpu.SemaphoreType.DMA((n,)),
            pltpu.SemaphoreType.DMA((n,)),
            pltpu.SemaphoreType.DMA((n,)),
            pltpu.SemaphoreType.DMA((n,)),
        ],
        compiler_params=pltpu.CompilerParams(
            collective_id=0, has_side_effects=True, vmem_limit_bytes=58 * 1024 * 1024
        ),
        name="expert_layer",
    )(tokens, expert_ids.T, slots.T, gates.T, gate_weight, up_weight, down_weight)


def solution(mesh):
    return jax.shard_map(
        body,
        mesh=mesh,
        in_specs=(
            P(("groups", "expert"), None),
            P("expert", None, None),
            P("expert", None, None),
            P("expert", None, None),
            P(("groups", "expert"), None),
            P(("groups", "expert"), None),
            P(("groups", "expert"), None),
        ),
        out_specs=P(("groups", "expert"), None),
        check_vma=False,
    )
```

```python
import functools

import jax
import jax.numpy as jnp
from jax import lax
from jax.experimental import pallas as pl
from jax.experimental.pallas import tpu as pltpu
from jax.sharding import PartitionSpec as P

EXPERTS = 16
CAP = 16
SENDS = ((8, 8), (4, 4), (0, 4))
WORKS = ((8, 4), (0, 8), (12, 2), (14, 2))
MIXES = ((0, 8), (8, 4), (12, 4))


def xor_index(a, b, n):
    out, bit = 0, 1
    while bit < n:
        out = out + ((a // bit + b // bit) % 2) * bit
        bit *= 2
    return out


def column_tile(width, most):
    tile = most
    while width % tile:
        tile //= 2
    return tile


def kernel(
    n, tokens_ref, ids_ref, slots_ref, gates_ref, gate_hbm, up_hbm, down_hbm, out_ref,
    gate_w, up_w, down_w, send, inbox, outbox, back, hidden, acc, pack, weight_sems,
    there_send, there_recv, back_send, back_recv,
):
    me = lax.axis_index("expert")
    shards = n // EXPERTS
    unit = n // EXPERTS
    token_count, width = tokens_ref.shape
    ff = gate_w.shape[1]
    top = ids_ref.shape[0]

    weights = [
        pltpu.make_async_copy(src.at[0], dst, weight_sems.at[i])
        for i, (src, dst) in enumerate(((gate_hbm, gate_w), (up_hbm, up_w), (down_hbm, down_w)))
    ]
    for copy in weights:
        copy.start()

    barrier = pltpu.get_barrier_semaphore()

    def greet(j, carry):
        pl.semaphore_signal(barrier, inc=1, device_id={"expert": xor_index(me, j, n)})
        return carry

    lax.fori_loop(1, n, greet, 0)

    target = jnp.where(slots_ref[...] >= 0, ids_ref[...] * CAP + slots_ref[...], -1)
    slot_row = lax.broadcasted_iota(jnp.int32, (EXPERTS * CAP, token_count), 0)
    chosen = jnp.zeros((EXPERTS * CAP, token_count), jnp.float32)
    for k in range(top):
        chosen = jnp.where(target[k : k + 1, :] == slot_row, 1.0, chosen)
    pack[...] = chosen.astype(jnp.bfloat16)
    tile_p = column_tile(width, 512)

    def pack_tile(i, carry):
        cols = pl.ds(pl.multiple_of(i * tile_p, tile_p), tile_p)
        send[:, cols] = jnp.dot(
            pack[...], tokens_ref[:, cols], preferred_element_type=jnp.float32
        ).astype(jnp.bfloat16)
        return carry

    lax.fori_loop(0, width // tile_p, pack_tile, 0)
    pl.semaphore_wait(barrier, n - 1)

    def block(j):
        return pl.ds(pl.multiple_of(j * CAP, CAP), CAP)

    def dispatch(j):
        peer = xor_index(me, j, n)
        return pltpu.make_async_remote_copy(
            src_ref=send.at[block(peer // shards)],
            dst_ref=inbox.at[block(j)],
            send_sem=there_send.at[j],
            recv_sem=there_recv.at[j],
            device_id={"expert": peer},
        )

    def giveback(j):
        return pltpu.make_async_remote_copy(
            src_ref=outbox.at[block(j)],
            dst_ref=back.at[block(j)],
            send_sem=back_send.at[j],
            recv_sem=back_recv.at[j],
            device_id={"expert": xor_index(me, j, n)},
        )

    def each(group, act):
        first, count = group[0] * unit, group[1] * unit

        def step(j, carry):
            act(j)
            return carry

        lax.fori_loop(max(first, 1), first + count, step, 0)

    for group in SENDS:
        each(group, lambda j: dispatch(j).start())
    inbox[0:CAP, :] = send[block(me // shards), :]

    tile_f = column_tile(ff, 256)
    tile_d = column_tile(width, 512)
    for place, group in enumerate(WORKS):
        start, rows = group[0] * unit * CAP, group[1] * unit * CAP
        mine = slice(start, start + rows)
        each(group, lambda j: dispatch(j).wait_recv())
        if place == 0:
            weights[0].wait()
            weights[1].wait()

        def first_half(i, carry):
            cols = pl.ds(pl.multiple_of(i * tile_f, tile_f), tile_f)
            gate_val = jnp.dot(
                inbox[mine, :], gate_w[:, cols], preferred_element_type=jnp.float32
            )
            up_val = jnp.dot(inbox[mine, :], up_w[:, cols], preferred_element_type=jnp.float32)
            hidden[:rows, cols] = (jax.nn.silu(gate_val) * up_val).astype(jnp.bfloat16)
            return carry

        lax.fori_loop(0, ff // tile_f, first_half, 0)
        if place == 0:
            weights[2].wait()

        def second_half(i, carry):
            cols = pl.ds(pl.multiple_of(i * tile_d, tile_d), tile_d)
            outbox[mine, cols] = jnp.dot(
                hidden[:rows, :], down_w[:, cols], preferred_element_type=jnp.float32
            ).astype(jnp.bfloat16)
            return carry

        lax.fori_loop(0, width // tile_d, second_half, 0)
        each(group, lambda j: giveback(j).start())
    back[0:CAP, :] = outbox[0:CAP, :]

    def mix_group(place, group):
        start, rows = group[0] * unit * CAP, group[1] * unit * CAP
        mine = slice(start, start + rows)
        row = lax.broadcasted_iota(jnp.int32, (rows, token_count), 0) + start
        expert = ((row // CAP) ^ me) // shards
        key = expert * CAP + row % CAP
        mix = jnp.zeros((rows, token_count), jnp.float32)
        for k in range(top):
            mix = jnp.where(target[k : k + 1, :] == key, gates_ref[k : k + 1, :], mix)
        mix = mix.T
        high = mix.astype(jnp.bfloat16)
        low = (mix - high.astype(jnp.float32)).astype(jnp.bfloat16)
        both = jnp.concatenate([high, low], axis=0)
        each(group, lambda j: giveback(j).wait_recv())

        def mix_tile(i, carry):
            cols = pl.ds(pl.multiple_of(i * tile_d, tile_d), tile_d)
            product = jnp.dot(both, back[mine, cols], preferred_element_type=jnp.float32)
            total = product[:token_count] + product[token_count:]
            if place > 0:
                total = total + acc[:, cols]
            if place < len(MIXES) - 1:
                acc[:, cols] = total
            else:
                out_ref[:, cols] = total.astype(jnp.bfloat16)
            return carry

        lax.fori_loop(0, width // tile_d, mix_tile, 0)

    for place, group in enumerate(MIXES):
        mix_group(place, group)
    each((0, EXPERTS), lambda j: dispatch(j).wait_send())
    each((0, EXPERTS), lambda j: giveback(j).wait_send())


def body(tokens, gate_weight, up_weight, down_weight, expert_ids, slots, gates):
    n = lax.axis_size("expert")
    token_count, width = tokens.shape
    ff = gate_weight.shape[2]
    rows = max(count for _, count in WORKS) * (n // EXPERTS) * CAP
    vmem = pl.BlockSpec(memory_space=pltpu.VMEM)
    hbm = pl.BlockSpec(memory_space=pl.ANY)
    return pl.pallas_call(
        functools.partial(kernel, n),
        out_shape=pltpu.VMEM((token_count, width), jnp.bfloat16),
        in_specs=[vmem] * 4 + [hbm] * 3,
        out_specs=vmem,
        scratch_shapes=[
            pltpu.VMEM((width, ff), jnp.bfloat16),
            pltpu.VMEM((width, ff), jnp.bfloat16),
            pltpu.VMEM((ff, width), jnp.bfloat16),
            pltpu.VMEM((EXPERTS * CAP, width), jnp.bfloat16),
            pltpu.VMEM((n * CAP, width), jnp.bfloat16),
            pltpu.VMEM((n * CAP, width), jnp.bfloat16),
            pltpu.VMEM((n * CAP, width), jnp.bfloat16),
            pltpu.VMEM((rows, ff), jnp.bfloat16),
            pltpu.VMEM((token_count, width), jnp.float32),
            pltpu.VMEM((EXPERTS * CAP, token_count), jnp.bfloat16),
            pltpu.SemaphoreType.DMA((3,)),
            pltpu.SemaphoreType.DMA((n,)),
            pltpu.SemaphoreType.DMA((n,)),
            pltpu.SemaphoreType.DMA((n,)),
            pltpu.SemaphoreType.DMA((n,)),
        ],
        compiler_params=pltpu.CompilerParams(
            collective_id=0, has_side_effects=True, vmem_limit_bytes=58 * 1024 * 1024
        ),
        name="expert_layer",
    )(tokens, expert_ids.T, slots.T, gates.T, gate_weight, up_weight, down_weight)


def solution(mesh):
    return jax.shard_map(
        body,
        mesh=mesh,
        in_specs=(
            P(("groups", "expert"), None),
            P("expert", None, None),
            P("expert", None, None),
            P("expert", None, None),
            P(("groups", "expert"), None),
            P(("groups", "expert"), None),
            P(("groups", "expert"), None),
        ),
        out_specs=P(("groups", "expert"), None),
        check_vma=False,
    )
```

```python
import functools

import jax
import jax.numpy as jnp
from jax import lax
from jax.experimental import pallas as pl
from jax.experimental.pallas import tpu as pltpu
from jax.sharding import PartitionSpec as P

EXPERTS = 16
CAP = 16
SENDS = ((8, 8), (0, 4), (4, 4))
WORKS = ((8, 4), (0, 8), (12, 2), (14, 2))
MIXES = ((0, 8), (8, 4), (12, 4))


def xor_index(a, b, n):
    out, bit = 0, 1
    while bit < n:
        out = out + ((a // bit + b // bit) % 2) * bit
        bit *= 2
    return out


def column_tile(width, most):
    tile = most
    while width % tile:
        tile //= 2
    return tile


def kernel(
    n, tokens_ref, ids_ref, slots_ref, gates_ref, gate_hbm, up_hbm, down_hbm, out_ref,
    gate_w, up_w, down_w, send, inbox, outbox, back, hidden, acc, pack, weight_sems,
    there_send, there_recv, back_send, back_recv,
):
    me = lax.axis_index("expert")
    shards = n // EXPERTS
    unit = n // EXPERTS
    token_count, width = tokens_ref.shape
    ff = gate_w.shape[1]
    top = ids_ref.shape[0]

    weights = [
        pltpu.make_async_copy(src.at[0], dst, weight_sems.at[i])
        for i, (src, dst) in enumerate(((gate_hbm, gate_w), (up_hbm, up_w), (down_hbm, down_w)))
    ]

    barrier = pltpu.get_barrier_semaphore()

    def greet(j, carry):
        pl.semaphore_signal(barrier, inc=1, device_id={"expert": xor_index(me, j, n)})
        return carry

    lax.fori_loop(1, n, greet, 0)

    target = jnp.where(slots_ref[...] >= 0, ids_ref[...] * CAP + slots_ref[...], -1)
    slot_row = lax.broadcasted_iota(jnp.int32, (EXPERTS * CAP, token_count), 0)
    chosen = jnp.zeros((EXPERTS * CAP, token_count), jnp.float32)
    for k in range(top):
        chosen = jnp.where(target[k : k + 1, :] == slot_row, 1.0, chosen)
    pack[...] = chosen.astype(jnp.bfloat16)
    tile_p = column_tile(width, 512)

    def pack_tile(i, carry):
        cols = pl.ds(pl.multiple_of(i * tile_p, tile_p), tile_p)
        send[:, cols] = jnp.dot(
            pack[...], tokens_ref[:, cols], preferred_element_type=jnp.float32
        ).astype(jnp.bfloat16)
        return carry

    lax.fori_loop(0, width // tile_p, pack_tile, 0)
    pl.semaphore_wait(barrier, n - 1)

    def block(j):
        return pl.ds(pl.multiple_of(j * CAP, CAP), CAP)

    def dispatch(j):
        peer = xor_index(me, j, n)
        return pltpu.make_async_remote_copy(
            src_ref=send.at[block(peer // shards)],
            dst_ref=inbox.at[block(j)],
            send_sem=there_send.at[j],
            recv_sem=there_recv.at[j],
            device_id={"expert": peer},
        )

    def giveback(j):
        return pltpu.make_async_remote_copy(
            src_ref=outbox.at[block(j)],
            dst_ref=back.at[block(j)],
            send_sem=back_send.at[j],
            recv_sem=back_recv.at[j],
            device_id={"expert": xor_index(me, j, n)},
        )

    def each(group, act):
        first, count = group[0] * unit, group[1] * unit

        def step(j, carry):
            act(j)
            return carry

        lax.fori_loop(max(first, 1), first + count, step, 0)

    for group in SENDS:
        each(group, lambda j: dispatch(j).start())
    for copy in weights:
        copy.start()
    inbox[0:CAP, :] = send[block(me // shards), :]

    tile_f = column_tile(ff, 256)
    tile_d = column_tile(width, 512)
    for place, group in enumerate(WORKS):
        start, rows = group[0] * unit * CAP, group[1] * unit * CAP
        mine = slice(start, start + rows)
        each(group, lambda j: dispatch(j).wait_recv())
        if place == 0:
            weights[0].wait()
            weights[1].wait()

        def first_half(i, carry):
            cols = pl.ds(pl.multiple_of(i * tile_f, tile_f), tile_f)
            gate_val = jnp.dot(
                inbox[mine, :], gate_w[:, cols], preferred_element_type=jnp.float32
            )
            up_val = jnp.dot(inbox[mine, :], up_w[:, cols], preferred_element_type=jnp.float32)
            hidden[:rows, cols] = (jax.nn.silu(gate_val) * up_val).astype(jnp.bfloat16)
            return carry

        lax.fori_loop(0, ff // tile_f, first_half, 0)
        if place == 0:
            weights[2].wait()

        def second_half(i, carry):
            cols = pl.ds(pl.multiple_of(i * tile_d, tile_d), tile_d)
            outbox[mine, cols] = jnp.dot(
                hidden[:rows, :], down_w[:, cols], preferred_element_type=jnp.float32
            ).astype(jnp.bfloat16)
            return carry

        lax.fori_loop(0, width // tile_d, second_half, 0)
        each(group, lambda j: giveback(j).start())
    back[0:CAP, :] = outbox[0:CAP, :]

    def mix_group(place, group):
        start, rows = group[0] * unit * CAP, group[1] * unit * CAP
        mine = slice(start, start + rows)
        row = lax.broadcasted_iota(jnp.int32, (rows, token_count), 0) + start
        expert = ((row // CAP) ^ me) // shards
        key = expert * CAP + row % CAP
        mix = jnp.zeros((rows, token_count), jnp.float32)
        for k in range(top):
            mix = jnp.where(target[k : k + 1, :] == key, gates_ref[k : k + 1, :], mix)
        mix = mix.T
        high = mix.astype(jnp.bfloat16)
        low = (mix - high.astype(jnp.float32)).astype(jnp.bfloat16)
        both = jnp.concatenate([high, low], axis=0)
        each(group, lambda j: giveback(j).wait_recv())

        def mix_tile(i, carry):
            cols = pl.ds(pl.multiple_of(i * tile_d, tile_d), tile_d)
            product = jnp.dot(both, back[mine, cols], preferred_element_type=jnp.float32)
            total = product[:token_count] + product[token_count:]
            if place > 0:
                total = total + acc[:, cols]
            if place < len(MIXES) - 1:
                acc[:, cols] = total
            else:
                out_ref[:, cols] = total.astype(jnp.bfloat16)
            return carry

        lax.fori_loop(0, width // tile_d, mix_tile, 0)

    for place, group in enumerate(MIXES):
        mix_group(place, group)
    each((0, EXPERTS), lambda j: dispatch(j).wait_send())
    each((0, EXPERTS), lambda j: giveback(j).wait_send())


def body(tokens, gate_weight, up_weight, down_weight, expert_ids, slots, gates):
    n = lax.axis_size("expert")
    token_count, width = tokens.shape
    ff = gate_weight.shape[2]
    rows = max(count for _, count in WORKS) * (n // EXPERTS) * CAP
    vmem = pl.BlockSpec(memory_space=pltpu.VMEM)
    hbm = pl.BlockSpec(memory_space=pl.ANY)
    return pl.pallas_call(
        functools.partial(kernel, n),
        out_shape=pltpu.VMEM((token_count, width), jnp.bfloat16),
        in_specs=[vmem] * 4 + [hbm] * 3,
        out_specs=vmem,
        scratch_shapes=[
            pltpu.VMEM((width, ff), jnp.bfloat16),
            pltpu.VMEM((width, ff), jnp.bfloat16),
            pltpu.VMEM((ff, width), jnp.bfloat16),
            pltpu.VMEM((EXPERTS * CAP, width), jnp.bfloat16),
            pltpu.VMEM((n * CAP, width), jnp.bfloat16),
            pltpu.VMEM((n * CAP, width), jnp.bfloat16),
            pltpu.VMEM((n * CAP, width), jnp.bfloat16),
            pltpu.VMEM((rows, ff), jnp.bfloat16),
            pltpu.VMEM((token_count, width), jnp.float32),
            pltpu.VMEM((EXPERTS * CAP, token_count), jnp.bfloat16),
            pltpu.SemaphoreType.DMA((3,)),
            pltpu.SemaphoreType.DMA((n,)),
            pltpu.SemaphoreType.DMA((n,)),
            pltpu.SemaphoreType.DMA((n,)),
            pltpu.SemaphoreType.DMA((n,)),
        ],
        compiler_params=pltpu.CompilerParams(
            collective_id=0, has_side_effects=True, vmem_limit_bytes=58 * 1024 * 1024
        ),
        name="expert_layer",
    )(tokens, expert_ids.T, slots.T, gates.T, gate_weight, up_weight, down_weight)


def solution(mesh):
    return jax.shard_map(
        body,
        mesh=mesh,
        in_specs=(
            P(("groups", "expert"), None),
            P("expert", None, None),
            P("expert", None, None),
            P("expert", None, None),
            P(("groups", "expert"), None),
            P(("groups", "expert"), None),
            P(("groups", "expert"), None),
        ),
        out_specs=P(("groups", "expert"), None),
        check_vma=False,
    )
```
